128 devices in a mesh: section: 2 (over core), ctx: 16 (over y, x), head: 4 (over z).
Axes of the slice: x: 4, y: 4, z: 4, core: 2. Of those that a mesh axis runs over, the one named last changes fastest.
Arguments:
- acts: bfloat16 [2, 2, 6144, 4096], P('section', None, 'ctx', 'head'), may hold values from -6 to 6
- w_qkv: bfloat16 [2, 4096, 3, 4096], P('section', 'ctx', None, 'head'), may hold values from -0.09375 to 0.09375
- w_gate: bfloat16 [2, 4096, 32], P('section', 'ctx', 'head'), may hold values from -0.1875 to 0.1875
- gate_bias: float32 [2, 32], P('section', 'head'), may hold values from -2 to 2
- decay_rate: float32 [2, 32], P('section', 'head'), may hold values from 3.2552083e-06 to 0.15
- norm_gain: float32 [2, 4096], P('section', 'head'), may hold values from 0.1 to 1.9
- w_out: bfloat16 [2, 4096, 4096], P('section', 'head'), may hold values from -0.09375 to 0.09375
Outputs:
- passed: bfloat16 [2, 2, 6144, 4096], P('section', None, 'ctx', 'head')
The draws below stay inside these ranges and needn't reach their ends.
All inputs are finite; a program needn't handle non-finite values.
Results may differ from the reference program's by a relative error of at most 0.0041.
Values may be sent and summed in bfloat16 or wider, within the bound.
No kernel may reach another device: no remote copies, remote signals or barrier semaphores. Data moves between devices by JAX's collectives and lax.ppermute only.
A program may use at most 128 MiB of HBM per device.

```python
import jax
import jax.numpy as jnp
from jax import lax

D = 4096
DH = 128
MB = 2
BLOCK = 64
HEADS = 32
LENGTH = 6144
SECTIONS = 2


def draw_decay_rate(key, part):
    key = jax.random.fold_in(key, 7)
    spread = jax.random.uniform(jax.random.fold_in(key, 1), (SECTIONS, HEADS), jnp.float32)
    lowest = jnp.log(0.2 / LENGTH)
    highest = jnp.log(0.15)
    rate = jnp.exp(lowest + spread * (highest - lowest))
    return rate.astype(jnp.float32)


def levels(rng, extent, pieces, low, high):
    def one(position, blocks):
        steps = jax.random.uniform(jax.random.fold_in(jax.random.fold_in(rng, 6), position), (blocks,), jnp.float32, low / len(pieces), high / len(pieces))
        return jnp.repeat(jnp.exp(steps), extent[position] // blocks).reshape((-1,) + (1,) * (len(extent) - position - 1))

    factor_of = one(*pieces[0])
    for cut in pieces[1:]:
        factor_of = factor_of * one(*cut)
    return factor_of


def scatter_about(key, dims, width, most, cuts=(), dtype=jnp.bfloat16):
    entries = width * jax.random.normal(key, dims, jnp.float32)
    if cuts:
        entries = entries * levels(key, dims, cuts, -0.22, 0.18)
    return jnp.clip(entries, -most, most).astype(dtype)


def setup_inputs(seed: int = 0) -> dict:
    seeds = jax.random.split(jax.random.key(seed), 8)
    return {
        "acts": scatter_about(seeds[0], (SECTIONS, MB, LENGTH, D), 1.0, 6.0, ((0, 2), (2, 16), (3, 4))),
        "w_qkv": scatter_about(seeds[1], (SECTIONS, D, 3, HEADS * DH), D ** -0.5, 0.09375, ((0, 2), (1, 16), (3, 4))),
        "w_gate": scatter_about(seeds[2], (SECTIONS, D, HEADS), (D // 4) ** -0.5, 0.1875, ((0, 2), (1, 16), (2, 4))),
        "gate_bias": jnp.clip(jax.random.uniform(seeds[3], (SECTIONS, HEADS), jnp.float32, -2.0, 2.0) * levels(seeds[3], (SECTIONS, HEADS), ((0, 2), (1, 4)), -0.4, 0.0), -2.0, 2.0),
        "decay_rate": draw_decay_rate(jax.random.fold_in(seeds[7], 71), 0),
        "norm_gain": jnp.clip(1.0 + 0.18 * jax.random.normal(seeds[5], (SECTIONS, HEADS * DH), jnp.float32), 0.1, 1.9),
        "w_out": scatter_about(seeds[6], (SECTIONS, HEADS * DH, D), (HEADS * DH) ** -0.5, 0.09375, ((0, 2), (1, 4))),
    }


PRECISION_TOP = lax.Precision.HIGHEST

def unit_rows(matrix):
    return matrix * lax.rsqrt(lax.optimization_barrier(jnp.sum(matrix * matrix, axis=-1, keepdims=True)) + 1e-06)

def block_step(query_tile, key_block, value_tile, decay_block, head_state):
    depth_level = jnp.cumsum(decay_block, axis=0)
    count = decay_block.shape[0]
    places = jnp.arange(count)
    lower = places[:, None] >= places[None, :]
    spread = depth_level[:, None, :] - depth_level[None, :, :]
    weights = jnp.where(lower[:, :, None], jnp.exp(jnp.minimum(spread, 0.0)), 0.0)
    scores = jnp.einsum('ihd,jhd->ijh', query_tile, key_block, precision=PRECISION_TOP) * weights
    inner = jnp.einsum('ijh,jhd->ihd', scores, value_tile, precision=PRECISION_TOP)
    carried_over = jnp.exp(depth_level)[:, :, None] * jnp.einsum('mje,jea->mja', query_tile, head_state, precision=PRECISION_TOP)
    final_state = depth_level[-1]
    decayed_keys = key_block * jnp.exp(final_state[None, :] - depth_level)[:, :, None]
    updated_state = jnp.exp(final_state)[:, None, None] * head_state + jnp.einsum('ego,egf->gof', decayed_keys, value_tile, precision=PRECISION_TOP)
    return (inner + carried_over, updated_state, depth_level)

def layer(inputs, weight_qkv, weight_gate, bias, rate, gain, weight_out):
    length = inputs.shape[0]
    projected = jnp.dot(inputs, weight_qkv.reshape(D, 3 * HEADS * DH), preferred_element_type=jnp.float32)
    projected = projected.reshape(length, 3, HEADS, DH)
    gate_terms = jnp.dot(inputs, weight_gate, preferred_element_type=jnp.float32)
    log_decay = -rate[None, :] * jax.nn.sigmoid(gate_terms + bias[None, :])
    queries = unit_rows(projected[:, 0])
    keys = unit_rows(projected[:, 1])
    values = projected[:, 2]
    blocks = length // BLOCK

    def advance(head_state, parts):
        outputs, updated_state, depth_level = block_step(parts[0], parts[1], parts[2], parts[3], head_state)
        return (updated_state, outputs)
    start_state = jnp.zeros((HEADS, DH, DH), jnp.float32)
    split = (queries.reshape(blocks, BLOCK, HEADS, DH), keys.reshape(blocks, BLOCK, HEADS, DH), values.reshape(blocks, BLOCK, HEADS, DH), log_decay.reshape(blocks, BLOCK, HEADS))
    ending, outputs = lax.scan(advance, start_state, split)
    outputs = outputs.reshape(length, HEADS, DH)
    normed = outputs * lax.rsqrt(lax.optimization_barrier(jnp.mean(outputs * outputs, axis=-1, keepdims=True)) + 1e-06)
    mixed = (normed.reshape(length, HEADS * DH) * gain[None, :]).astype(jnp.bfloat16)
    total = inputs.astype(jnp.float32) + jnp.dot(mixed, weight_out, preferred_element_type=jnp.float32)
    return total.astype(jnp.bfloat16)

def reference(acts, w_qkv, w_gate, gate_bias, decay_rate, norm_gain, w_out):
    layered = []
    for section in range(SECTIONS):
        batch_list = []
        for batch in range(MB):
            batch_list.append(layer(acts[section, batch], w_qkv[section], w_gate[section], gate_bias[section], decay_rate[section], norm_gain[section], w_out[section]))
        layered.append(jnp.stack(batch_list))
    layered = jnp.stack(layered)
    return jnp.roll(layered, 1, axis=0)
```

```python
import functools

import jax
import jax.numpy as jnp
from jax import lax
from jax.experimental import pallas as pl
from jax.experimental.pallas import tpu as pltpu
from jax.sharding import PartitionSpec as P

SIDE = 4
DH = 128
F32 = jnp.float32
BF16 = jnp.bfloat16
HALVES = ((0, 1, 2, 3), (4, 5, 6, 7))
GATE_ROWS = 16
VMEM = 48 * 1024 * 1024


def send(block, dy, dx):
    pairs = [
        (y * SIDE + x, ((y + dy) % SIDE) * SIDE + (x + dx) % SIDE)
        for y in range(SIDE)
        for x in range(SIDE)
    ]
    return lax.ppermute(block, "ctx", pairs)


def send_head(block, distance):
    return lax.ppermute(block, "head", [(i, (i + distance) % SIDE) for i in range(SIDE)])


def tied(value, *others):
    return lax.optimization_barrier((value, others))[0]


def swing(block, axis, turn):
    size = lax.axis_size("head" if axis == "z" else "ctx")
    pairs = []
    for section in (0, 1):
        step = (turn if section == 0 else -turn) % SIDE
        for i in range(size):
            y, x = divmod(i, SIDE)
            to = {"x": y * SIDE + (x + step) % SIDE, "y": (y + step) % SIDE * SIDE + x, "z": (i + step) % SIDE}[axis]
            pairs.append((section * size + i, section * size + to))
    return lax.ppermute(block, ("section", "head" if axis == "z" else "ctx"), pairs)


def ring(block, axis):
    one, three = swing(block, axis, 1), swing(block, axis, -1)
    return block, one, swing(one, axis, 1), three


def far_ring(low, high, axis, late):
    low_one, low_three = swing(low, axis, 1), swing(low, axis, -1)
    high_one, high_three = swing(tied(high, low_one), axis, 1), swing(tied(high, low_three), axis, -1)
    low_two, high_two = tied((low_one, high_one), low_three, high_three, *late)
    return (low, high), (low_one, high_one), (swing(low_two, axis, 1), swing(high_two, axis, 1)), (low_three, high_three)


def copy_kernel(index_ref, in_ref, out_ref):
    out_ref[...] = in_ref[...].reshape(out_ref.shape)


def reorder(array, index, grid, in_block, in_map, out_block, out_map, out_shape):
    return pl.pallas_call(
        copy_kernel,
        grid_spec=pltpu.PrefetchScalarGridSpec(
            num_scalar_prefetch=1,
            grid=grid,
            in_specs=[pl.BlockSpec(in_block, in_map)],
            out_specs=pl.BlockSpec(out_block, out_map),
        ),
        out_shape=jax.ShapeDtypeStruct(out_shape, array.dtype),
        compiler_params=pltpu.CompilerParams(vmem_limit_bytes=VMEM),
        cost_estimate=pl.CostEstimate(flops=0, bytes_accessed=2 * array.size * 2, transcendentals=0),
        name="reorder",
    )(index, array)


def in_two(a):
    high = a.astype(BF16)
    return high, (a - high.astype(F32)).astype(BF16)


def product(a, b, at):
    return lax.dot_general(a, b, (at, ((), ())), preferred_element_type=F32)


def times_pair(a, b, b_high, dims):
    high, low = in_two(a)
    both = product(high, b, dims)
    return both[:, :DH] + (both[:, DH:] + product(low, b_high, dims))


def attend(q, k, v, level, mask):
    count = level.shape[0]
    middle = level[count // 2 - 1 : count // 2]
    final = level[count - 1 : count]
    q = q * lax.rsqrt(jnp.sum(q * q, axis=1, keepdims=True) + 1e-06)
    k = k * lax.rsqrt(jnp.sum(k * k, axis=1, keepdims=True) + 1e-06)
    q_high, q_low = in_two(q * jnp.exp(level - middle))
    k_high, k_low = in_two(k * jnp.exp(middle - level))
    last = ((1,), (1,))
    scores = product(
        jnp.concatenate([q_high, q_high], axis=1), jnp.concatenate([k_high, k_low], axis=1), last
    ) + product(q_low, k_high, last)
    scores = jnp.where(mask, scores, 0.0)
    v_high, v_low = in_two(v)
    pair = jnp.concatenate([v_high, v_low], axis=1)
    outputs = times_pair(scores, pair, v_high, ((1,), (0,)))
    state = times_pair(k * jnp.exp(final - level), pair, v_high, ((0,), (0,)))
    return outputs, (q * jnp.exp(level)).astype(BF16), state.astype(BF16)


def wide(ref):
    return jnp.concatenate([ref[j] for j in range(ref.shape[0])], axis=1)


def times(x, w):
    return lax.dot_general(x, w, (((1,), (1,)), ((), ())), preferred_element_type=F32)


def x_specs(x, half, blocks):
    tokens, width = x.shape[1:]

    def spec(k, j):
        dy, dx = (k, j) if half == 0 else (j, k)

        def at_block(h, at):
            slot = lax.rem(at[3] * (lax.rem(at[1] + at[3] * dy, SIDE) + SIDE - at[2]), SIDE)
            return slot, 0, lax.rem(at[0] + at[3] * dx, SIDE)

        return pl.BlockSpec((1, tokens, width // SIDE), at_block)

    return [spec(k, j) for k, j in blocks]


def side_by_side(refs):
    return jnp.concatenate([ref[0] for ref in refs], axis=1)


def near_kernel(at_ref, *refs):
    w_refs, out_ref = refs[-7:-1], refs[-1]
    total = 0.0
    for i in range(3):
        w = jnp.concatenate([wide(w_refs[2 * i]), wide(w_refs[2 * i + 1])], axis=1)
        total = total + times(side_by_side(refs[SIDE * i : SIDE * (i + 1)]), w)
    out_ref[...] = total


def near_product(place, x, half, blocks, n):
    tokens, width = x.shape[1:]
    size = 6 * DH
    w_spec = pl.BlockSpec((SIDE // 2, size, blocks[0][0].shape[2]), lambda h, at: (0, h, 0))
    specs = x_specs(x, half, [(k, j) for k in (0, 1, 3) for j in range(SIDE)])
    return pl.pallas_call(
        near_kernel,
        grid_spec=pltpu.PrefetchScalarGridSpec(
            num_scalar_prefetch=1,
            grid=(n // 2,),
            in_specs=specs + [w_spec] * 6,
            out_specs=pl.BlockSpec((tokens, size), lambda h, at: (0, h)),
        ),
        out_shape=jax.ShapeDtypeStruct((tokens, 3 * DH * n), F32),
        compiler_params=pltpu.CompilerParams(vmem_limit_bytes=VMEM),
        cost_estimate=pl.CostEstimate(
            flops=2 * 3 * tokens * width * 3 * DH * n, bytes_accessed=3 * tokens * width * 2 * 2, transcendentals=0
        ),
        name="near_product",
    )(place, *[x] * len(specs), *[part for k in (0, 1, 3) for part in blocks[k]])


def gate_product(x_refs, w_refs):
    total = 0.0
    for w_ref in w_refs:
        parts, x_refs = x_refs[: w_ref.shape[0]], x_refs[w_ref.shape[0] :]
        total = total + times(side_by_side(parts), wide(w_ref))
    return total


def gate_near_kernel(at_ref, *refs):
    count = 3 * SIDE
    refs[-1][...] = gate_product(refs[:count], refs[count:-1])


def gate_kernel(at_ref, *refs):
    near_ref, bias_ref, rate_ref, out_ref = refs[-4:]
    total = near_ref[...] + gate_product(refs[:SIDE], refs[SIDE:-4])
    total = jnp.concatenate([total, jnp.zeros((total.shape[0], DH - GATE_ROWS), F32)], axis=1)
    log = -rate_ref[...] * jax.nn.sigmoid(total + bias_ref[...])
    count = out_ref.shape[1]
    row = lax.broadcasted_iota(jnp.int32, (count, count), 0)
    col = lax.broadcasted_iota(jnp.int32, (count, count), 1)
    lower = jnp.where(row >= col, 1.0, 0.0).astype(BF16)
    for b in range(out_ref.shape[0]):
        rest = log[b * count : (b + 1) * count]
        level = jnp.zeros_like(rest)
        for _ in range(3):
            term = rest.astype(BF16)
            rest = rest - term.astype(F32)
            level = level + jnp.dot(lower, term, preferred_element_type=F32)
        out_ref[b] = level


def gate_call(kernel, place, x, blocks, ks, rows, extra, shape, name):
    row = rows // GATE_ROWS
    specs = x_specs(x, 0, [(k, j) for k in ks for j in range(SIDE)])
    w = [part for k in ks for part in blocks[k]]
    whole = lambda v: pl.BlockSpec(v, lambda i, at: (0,) * len(v))
    return pl.pallas_call(
        kernel,
        grid_spec=pltpu.PrefetchScalarGridSpec(
            num_scalar_prefetch=1,
            grid=(1,),
            in_specs=specs
            + [pl.BlockSpec((part.shape[0], GATE_ROWS, part.shape[2]), lambda i, at: (0, row, 0)) for part in w]
            + [whole(v.shape) for v in extra],
            out_specs=whole(shape),
        ),
        out_shape=jax.ShapeDtypeStruct(shape, F32),
        compiler_params=pltpu.CompilerParams(vmem_limit_bytes=VMEM),
        cost_estimate=pl.CostEstimate(flops=10**9, bytes_accessed=len(ks) * 1572864, transcendentals=0),
        name=name,
    )(place, *[x] * len(specs), *w, *extra)


def local_kernel(heads, at_ref, *refs):
    x_refs, (w1_ref, w2_ref, near_ref, level_ref, o_ref, qe_ref, s_ref) = refs[:SIDE], refs[SIDE:]
    batches, count = level_ref.shape[:2]
    proj = near_ref[...] + times(
        side_by_side(x_refs), jnp.concatenate([wide(w1_ref), wide(w2_ref)], axis=1)
    )
    part = DH // SIDE
    places = (count, count)
    mask = lax.broadcasted_iota(jnp.int32, places, 0) >= lax.broadcasted_iota(jnp.int32, places, 1)
    for h in range(proj.shape[1] // (3 * DH)):
        pick = heads[0] + 2 * pl.program_id(0) + h
        column = slice(h * DH, (h + 1) * DH)
        for b in range(batches):
            rows = slice(b * count, (b + 1) * count)
            level = level_ref[b]
            lane = lax.broadcasted_iota(jnp.int32, level.shape, 1)
            level = jnp.sum(jnp.where(lane == pick, level, 0.0), axis=1, keepdims=True)
            q, k, v = (proj[rows, (3 * h + i) * DH : (3 * h + i + 1) * DH] for i in range(3))
            o_ref[rows, column], qe_ref[rows, column], state = attend(q, k, v, level, mask)
            for quarter in range(SIDE):
                to = slice((h * batches + b) * part, (h * batches + b + 1) * part)
                s_ref[quarter, to, :] = state[quarter * part : (quarter + 1) * part]


def local_pass(place, x, half, far, near, levels, heads):
    n = len(heads)
    batches, count = levels.shape[:2]
    tokens, width = x.shape[1:]
    w_spec = pl.BlockSpec((SIDE // 2, 6 * DH, far[0].shape[2]), lambda h, at: (0, h, 0))
    column = pl.BlockSpec((tokens, 2 * DH), lambda h, at: (0, h))
    part = 2 * batches * DH // SIDE
    return pl.pallas_call(
        functools.partial(local_kernel, heads),
        grid_spec=pltpu.PrefetchScalarGridSpec(
            num_scalar_prefetch=1,
            grid=(n // 2,),
            in_specs=x_specs(x, half, [(2, j) for j in range(SIDE)])
            + [
                w_spec,
                w_spec,
                pl.BlockSpec((tokens, 6 * DH), lambda h, at: (0, h)),
                pl.BlockSpec(levels.shape, lambda h, at: (0, 0, 0)),
            ],
            out_specs=[column, column, pl.BlockSpec((SIDE, part, DH), lambda h, at: (0, h, 0))],
        ),
        out_shape=[
            jax.ShapeDtypeStruct((tokens, n * DH), F32),
            jax.ShapeDtypeStruct((tokens, n * DH), BF16),
            jax.ShapeDtypeStruct((SIDE, n // 2 * part, DH), BF16),
        ],
        compiler_params=pltpu.CompilerParams(vmem_limit_bytes=VMEM),
        cost_estimate=pl.CostEstimate(
            flops=n * (2 * tokens * width * 3 * DH + batches * 60 * 2 * DH**3),
            bytes_accessed=n * tokens * DH * 20,
            transcendentals=0,
        ),
        name="local_pass",
    )(place, *[x] * SIDE, far[0], far[1], near, levels)


def lane_value(vector, lane):
    places = lax.broadcasted_iota(jnp.int32, vector.shape, 1)
    return jnp.sum(jnp.where(places == lane, vector, 0.0), axis=1, keepdims=True)


def write_logs(ref, logs):
    row = lax.broadcasted_iota(jnp.int32, (16, DH), 0)
    tail = jnp.zeros((16, DH), F32)
    for i in range(3):
        term = logs.astype(BF16).astype(F32)
        logs = logs - term
        tail = jnp.where(row == i, term, tail)
    ref[ref.shape[0] - 16 :, :] = tail.astype(BF16)


def read_logs(ref):
    return jnp.sum(ref[ref.shape[0] - 16 :, :].astype(F32), axis=0, keepdims=True)


def pack_kernel(heads, place_ref, s0_ref, s1_ref, level_ref, *out_refs):
    batches, count = level_ref.shape[:2]
    size = s0_ref.shape[1]
    lane = lax.broadcasted_iota(jnp.int32, (1, DH), 1)
    logs = jnp.zeros((1, DH), F32)
    last = [level_ref[b, count - 1 :, :] for b in range(batches)]
    for i, head in enumerate(heads):
        for b in range(batches):
            logs = jnp.where(lane == i * batches + b, lane_value(last[b], head), logs)
    for d, out_ref in enumerate(out_refs):
        quarter = lax.rem(place_ref[0] + SIDE - d, SIDE)
        out_ref[:size, :] = s0_ref[quarter]
        out_ref[size : 2 * size, :] = s1_ref[quarter]
        write_logs(out_ref, logs)


def after_place(logs, places, place, stop):
    total = jnp.zeros_like(logs[0])
    for log, other in zip(logs, places):
        total = total + jnp.where((other > place) & (other < stop), log, 0.0)
    return total


def rows_of(c):
    return slice(c * (DH // SIDE), (c + 1) * (DH // SIDE))


def row_kernel(count, place_ref, *refs):
    out_ref = refs[-1]
    places = [lax.rem(place_ref[0] + d, SIDE) for d in range(SIDE)]
    logs = [read_logs(ref) for ref in refs[:-1]]
    weights = [jnp.exp(after_place(logs, places, place, SIDE)) for place in places]
    for c in range(count):
        total = jnp.zeros((DH // SIDE, DH), F32)
        for d in range(SIDE):
            total = total + lane_value(weights[d], c) * refs[d][rows_of(c), :].astype(F32)
        out_ref[rows_of(c), :] = total.astype(BF16)
    write_logs(out_ref, logs[0] + logs[1] + logs[2] + logs[3])


def start_kernel(count, place_ref, *refs):
    x_refs, y_refs, out_refs = refs[:SIDE], refs[SIDE : 2 * SIDE - 1], refs[2 * SIDE - 1 :]
    x, y = place_ref[0], place_ref[1]
    places = [lax.rem(x + d, SIDE) for d in range(SIDE)]
    rows_at = [lax.rem(y + d, SIDE) for d in range(1, SIDE)]
    logs = [read_logs(ref) for ref in x_refs]
    row_logs = [read_logs(ref) for ref in y_refs]
    above = [jnp.where(at < y, jnp.exp(after_place(row_logs, rows_at, at, y)), 0.0) for at in rows_at]
    targets = [lax.rem(x + SIDE - d, SIDE) for d in range(SIDE)]
    passed = [jnp.exp(after_place(logs, places, -1, target)) for target in targets]
    inside = [
        [jnp.where(p < target, jnp.exp(after_place(logs, places, p, target)), 0.0) for p in places]
        for target in targets
    ]
    for c in range(count):
        start = sum(lane_value(w, c) * ref[rows_of(c), :].astype(F32) for w, ref in zip(above, y_refs))
        own = [ref[rows_of(c), :].astype(F32) for ref in x_refs]
        for t, out_ref in enumerate(out_refs):
            state = lane_value(passed[t], c) * start
            state = state + sum(lane_value(w, c) * block for w, block in zip(inside[t], own))
            out_ref[rows_of(c), :] = state.astype(BF16)


def small_call(kernel, place, arrays, shapes, name):
    return pl.pallas_call(
        kernel,
        in_specs=[pl.BlockSpec(memory_space=pltpu.SMEM)] + [pl.BlockSpec(memory_space=pltpu.VMEM)] * len(arrays),
        out_specs=[pl.BlockSpec(memory_space=pltpu.VMEM)] * len(shapes),
        out_shape=[jax.ShapeDtypeStruct(shape, BF16) for shape in shapes],
        compiler_params=pltpu.CompilerParams(vmem_limit_bytes=VMEM),
        cost_estimate=pl.CostEstimate(flops=10**6, bytes_accessed=10**6, transcendentals=0),
        name=name,
    )(place, *arrays)


def incoming_states(states, levels, heads, place):
    count = len(heads) * levels.shape[0]
    size = 2 * states[0].shape[1]
    shape = (size + 16, DH)
    messages = small_call(
        functools.partial(pack_kernel, heads), place, [*states, levels], [shape] * SIDE, "pack"
    )
    row = [messages[0]] + [send(messages[d], 0, -d) for d in (1, 2, 3)]
    (total,) = small_call(functools.partial(row_kernel, count), place, row, [shape], "row_sum")
    rows = [send(total, -d, 0) for d in (1, 2, 3)]
    parts = small_call(functools.partial(start_kernel, count), place, row + rows, [(size, DH)] * SIDE, "range_start")
    return [parts[0]] + [send(parts[d], 0, -d) for d in (1, 2, 3)]


def finish_kernel(halves, place_ref, *refs):
    o_refs, qe_refs, parts = refs[:2], refs[2:4], refs[4:8]
    gain_ref, far_w_ref, out_ref, far_ref = refs[8:]
    step = DH // SIDE
    n = o_refs[0].shape[1] // DH
    batches = parts[0].shape[0] // (halves * n * step)
    count = o_refs[0].shape[0] // batches
    here = [[lax.rem(place_ref[0] + d, SIDE) == q for d in range(1, SIDE)] for q in range(SIDE)]
    for half in range(halves):
        for h in range(n):
            column = slice((half * n + h) * DH, (half * n + h + 1) * DH)
            own = slice(h * DH, (h + 1) * DH)
            for b in range(batches):
                at = ((half * n + h) * batches + b) * step
                found = [ref[at : at + step, :].astype(F32) for ref in parts]
                quarters = []
                for q in range(SIDE):
                    quarter = found[0]
                    for d in range(1, SIDE):
                        quarter = jnp.where(here[q][d - 1], found[d], quarter)
                    quarters.append(quarter)
                state = jnp.concatenate(quarters, axis=0).astype(BF16)
                rows = slice(b * count, (b + 1) * count)
                o = o_refs[half][rows, own] + jnp.dot(
                    qe_refs[half][rows, own], state, preferred_element_type=F32
                )
                o = o * lax.rsqrt(jnp.mean(o * o, axis=1, keepdims=True) + 1e-06)
                out_ref[rows, column] = (o * gain_ref[:, column]).astype(BF16)
    far_ref[...] = jnp.dot(out_ref[...], far_w_ref[...], preferred_element_type=F32).astype(BF16)


def finish(local, parts, gain, place, far_w):
    whole = pl.BlockSpec(memory_space=pltpu.VMEM)
    arrays = [entry[0] for entry in local] + [entry[1] for entry in local] + list(parts) + [gain, far_w]
    tokens = local[0][0].shape[0]
    return pl.pallas_call(
        functools.partial(finish_kernel, len(local)),
        in_specs=[pl.BlockSpec(memory_space=pltpu.SMEM)] + [whole] * len(arrays),
        out_specs=[whole, whole],
        out_shape=[
            jax.ShapeDtypeStruct((tokens, gain.shape[1]), BF16),
            jax.ShapeDtypeStruct((tokens, far_w.shape[1]), BF16),
        ],
        compiler_params=pltpu.CompilerParams(vmem_limit_bytes=VMEM),
        cost_estimate=pl.CostEstimate(
            flops=2 * tokens * gain.shape[1] * DH, bytes_accessed=tokens * gain.shape[1] * 8, transcendentals=0
        ),
        name="finish",
    )(place, *arrays)


def body(acts, w_qkv, w_gate, gate_bias, decay_rate, norm_gain, w_out):
    x_local = acts[0]
    batches, tok, width = x_local.shape
    tokens = batches * tok
    heads = decay_rate.shape[1]
    ctx = lax.axis_index("ctx")
    y, x = ctx // SIDE, ctx % SIDE
    z = lax.axis_index("head")
    rows = w_qkv.shape[1]
    flat = x_local.reshape(tokens, width)

    weight = w_qkv[0].reshape(rows, 3, heads, DH).transpose(2, 1, 3, 0)
    gate_rows = jnp.pad(w_gate[0].T, ((0, GATE_ROWS - heads), (0, 0)))
    axes = ("x", "y")
    sources = [jnp.concatenate([weight[h].reshape(3 * DH, rows) for h in half], axis=0) for half in HALVES]
    sources[0] = jnp.concatenate([sources[0], gate_rows], axis=0)
    near = [ring(sources[half], axes[half]) for half in (0, 1)]

    sense = 3 - 2 * lax.axis_index("section")
    place = jnp.stack([x, y, z, sense]).astype(jnp.int32)
    w_rel = reorder(
        w_out[0], place, (SIDE,), (heads * DH, width), lambda i, at: (0, (at[2] + i) % SIDE),
        (1, heads * DH, width), lambda i, at: (i, 0, 0), (SIDE, heads * DH, width),
    )

    one = swing(flat, "z", 1)
    three = swing(tied(flat, one), "z", -1)
    two = swing(tied(one, three, w_rel), "z", 1)
    whole = jnp.stack([flat, one, two, three])

    both = (0, 1)
    stacks = [jnp.stack(blocks[at : at + 2]) for blocks in near for at in (0, 2)]
    gathered = [
        far_ring(stacks[2 * half], stacks[2 * half + 1], axes[1 - half], (whole,)) for half in both
    ]
    close = [near_product(place, whole, half, gathered[half], len(HALVES[half])) for half in both]
    at_gate = 3 * DH * len(HALVES[0])
    pad = lambda v: jnp.pad(v, ((0, 0), (0, DH - heads)))
    gate_near = gate_call(
        gate_near_kernel, place, whole, gathered[0], (0, 1, 3), at_gate, (), (tokens, GATE_ROWS), "gate_near"
    )
    levels = gate_call(
        gate_kernel, place, whole, gathered[0], (2,), at_gate,
        (tied(gate_near, *close), pad(gate_bias), pad(decay_rate)), (batches, tok, DH), "gate_levels",
    )
    local = [
        local_pass(place, whole, half, gathered[half][2], close[half], levels, HALVES[half]) for half in both
    ]
    parts = incoming_states([entry[2] for entry in local], levels, HALVES[0] + HALVES[1], place)
    mixed, far = finish(local, parts, norm_gain, place, w_rel[2])

    def partial_sum(rel):
        return jnp.dot(mixed, w_rel[rel], preferred_element_type=F32)

    from_low = send_head(far[:tok], 1)
    from_high = send_head(far[tok:], -1)
    up, down = partial_sum(1), partial_sum(3)
    up_late = send_head(up[tok:].astype(BF16), 1)
    down_early = send_head(down[:tok].astype(BF16), -1)
    up_early = send_head((up[:tok] + from_low.astype(F32)).astype(BF16), 1)
    down_late = send_head((down[tok:] + from_high.astype(F32)).astype(BF16), -1)
    mine = partial_sum(0) + flat.astype(F32)
    out = []
    for cut, one, two in ((slice(0, tok), down_early, up_early), (slice(tok, None), up_late, down_late)):
        layered = (mine[cut] + one.astype(F32) + two.astype(F32)).astype(BF16)
        out.append(lax.ppermute(layered, "section", [(0, 1), (1, 0)]))
    return jnp.stack(out)[None]


def solution(mesh):
    return jax.shard_map(
        body,
        mesh=mesh,
        in_specs=(
            P("section", None, "ctx", "head"),
            P("section", "ctx", None, "head"),
            P("section", "ctx", "head"),
            P("section", "head"),
            P("section", "head"),
            P("section", "head"),
            P("section", "head", None),
        ),
        out_specs=P("section", None, "ctx", "head"),
        check_vma=False,
    )
```
